256 devices in a mesh: lat: 4 (over z_hi), lon: 32 (over y, x, core), inner: 2 (over z_lo).
Axes of the slice: x: 4, y: 4, z: 8 (z_hi: 4, z_lo: 2; z = z_hi * 2 + z_lo), core: 2. Of those that a mesh axis runs over, the one named last changes fastest.
Arguments:
- tokens: bfloat16 [128, 2048, 512], P(('lat', 'inner'), 'lon'), may hold values from -6 to 6
- offsets: int32 [2], replicated, may hold values from 1 to 7, as said below
- regions: int32 [128, 2048], P(('lat', 'inner'), 'lon'), may hold values from 0 to 2
- norm_gain: float32 [512], replicated, may hold values from 0.25 to 1.75
- w_qkv: bfloat16 [512, 1536], replicated
- w_proj: bfloat16 [512, 512], replicated, may hold values from -0.25 to 0.25
- w_merge: bfloat16 [2048, 1024], replicated, may hold values from -0.125 to 0.125
- coarse_gain: float32 [1024], replicated, may hold values from 0.25 to 1.75
- w_in: bfloat16 [1024, 4096], P('lon', 'inner'), may hold values from -0.1875 to 0.1875
- w_out: bfloat16 [4096, 1024], P('inner', 'lon'), may hold values from -0.09375 to 0.09375
Outputs:
- fine_out: bfloat16 [128, 2048, 512], P(('lat', 'inner'), 'lon')
- coarse_out: bfloat16 [64, 1024, 1024], P(('lat', 'inner'), 'lon')
The draws below stay inside these ranges and needn't reach their ends.
Inputs may be any that keep to these rules, and one draw needn't show every extreme that they name: One of the two offsets is 7.
All inputs are finite; a program needn't handle non-finite values.
Results may differ from the reference program's by a relative error of at most 0.015.
The reference program's roundings to bfloat16 on the way (of `normed`, `packed`, `probs`, `mixed`, `grouped`, `coarse`, `coarse_normed` and `hidden`) count: a program that leaves them out, or rounds other values in their place, can miss the bound.
Values may be sent and summed in bfloat16 or wider, within the bound.
No kernel may reach another device: no remote copies, remote signals or barrier semaphores. Data moves between devices by JAX's collectives and lax.ppermute only.
A program may use at most 128 MiB of HBM per device.

```python
import jax
import jax.numpy as jnp
from jax import lax

C = 512
HEADS = 8
HEAD_DIM = 64
CC = 1024
FFC = 4096
W = 8
NLAT = 128
NLON = 2048


def draw_offsets(key, part):
    key = jax.random.fold_in(key, 5)
    first_key, second_key = jax.random.split(key)
    other = jax.random.randint(first_key, (), 1, W)
    flip = jax.random.randint(second_key, (), 0, 2)
    largest = jnp.int32(W - 1)
    return jnp.where(flip == 1, jnp.stack([largest, other]), jnp.stack([other, largest])).astype(jnp.int32)


def draw_w_qkv(key, part):
    key = jax.random.fold_in(key, 11)
    base = jax.random.normal(key, (C, 3 * C), jnp.float32) * C ** (-0.5)
    return base.astype(jnp.bfloat16)


def set_ends(array, own_key, low, high):
    place = [jax.random.randint(jax.random.fold_in(own_key, axis), (), 0, length) for axis, length in enumerate(array.shape)]
    longest = array.shape.index(max(array.shape))
    neighbour = place[:longest] + [(place[longest] + 1) % array.shape[longest]] + place[longest + 1:]
    return array.at[tuple(place)].set(low).at[tuple(neighbour)].set(high)


def block_levels(key, extent, cuts, low, high):
    level, own = 1.0, jax.random.fold_in(key, 6)
    for dim, parts in cuts:
        steps = jnp.exp(jax.random.uniform(jax.random.fold_in(own, dim), (parts,), jnp.float32, low / len(cuts), high / len(cuts)))
        level = level * jnp.repeat(steps, extent[dim] // parts).reshape([-1 if axis == dim else 1 for axis in range(len(extent))])
    return level


def gaussian(stream_key, shape, deviation, reach, cuts=(), dtype=jnp.bfloat16):
    array = deviation * jax.random.normal(stream_key, shape, jnp.float32)
    if cuts:
        array = array * block_levels(stream_key, shape, cuts, -0.22, 0.18)
    return jnp.clip(array, -reach, reach).astype(dtype)


def setup_inputs(seed: int = 0) -> dict:
    keys = jax.random.split(jax.random.key(seed), 11)
    tokens = gaussian(keys[0], (NLAT, NLON, C), 1.0, 6.0, ((0, 8), (1, 32)))
    offsets = draw_offsets(jax.random.fold_in(keys[10], 71), 0)
    regions = set_ends(jax.random.randint(keys[2], (NLAT, NLON), 0, 3), jax.random.fold_in(keys[2], 1), 0, 2).astype(jnp.int32)
    norm_gain = jnp.clip(1.0 + 0.15 * jax.random.normal(keys[3], (C,), jnp.float32), 0.25, 1.75)
    w_qkv = draw_w_qkv(jax.random.fold_in(keys[10], 71), 0)
    w_proj = gaussian(keys[5], (C, C), C ** -0.5, 0.25)
    w_merge = gaussian(keys[6], (4 * C, CC), (4 * C) ** -0.5, 0.125)
    coarse_gain = jnp.clip(1.0 + 0.15 * jax.random.normal(keys[7], (CC,), jnp.float32), 0.25, 1.75)
    w_in = gaussian(keys[8], (CC, FFC), CC ** -0.5, 0.1875, ((0, 32), (1, 2)))
    w_out = gaussian(keys[9], (FFC, CC), FFC ** -0.5, 0.09375, ((0, 2), (1, 32)))
    return {"tokens": tokens, "offsets": offsets, "regions": regions, "norm_gain": norm_gain, "w_qkv": w_qkv, "w_proj": w_proj, "w_merge": w_merge, "coarse_gain": coarse_gain, "w_in": w_in, "w_out": w_out}


def layer_norm(values, gain):
    values = values.astype(jnp.float32)
    center = values - lax.optimization_barrier(jnp.mean(values, axis=-1, keepdims=True))
    spread = lax.optimization_barrier(jnp.mean(center * center, axis=-1, keepdims=True))
    return center * lax.rsqrt(spread + 1e-05) * gain

def plain_norm(values):
    values = values.astype(jnp.float32)
    center = values - lax.optimization_barrier(jnp.mean(values, axis=-1, keepdims=True))
    spread = lax.optimization_barrier(jnp.mean(center * center, axis=-1, keepdims=True))
    return center * lax.rsqrt(spread + 1e-05)

def attend(packed, labels):
    count = packed.shape[0]
    width = packed.shape[-1] // 3
    queries = packed[..., :width].reshape(count, W * W, HEADS, HEAD_DIM).astype(jnp.float32)
    keys_all = packed[..., width:2 * width].reshape(count, W * W, HEADS, HEAD_DIM).astype(jnp.float32)
    values_all = packed[..., 2 * width:].reshape(count, W * W, HEADS, HEAD_DIM).astype(jnp.float32)
    scores = jnp.einsum('nqhd,nkhd->nhqk', queries, keys_all) / jnp.sqrt(jnp.float32(HEAD_DIM))
    allowed = labels[:, None, :, None] == labels[:, None, None, :]
    scores = jnp.where(allowed, scores, jnp.float32(-1e+30))
    scores = scores - lax.optimization_barrier(jnp.max(scores, axis=-1, keepdims=True))
    weights = jnp.exp(scores)
    probs = (weights / lax.optimization_barrier(jnp.sum(weights, axis=-1, keepdims=True))).astype(jnp.bfloat16)
    mixed = jnp.einsum('nhqk,nkhd->nqhd', probs.astype(jnp.float32), values_all)
    return mixed.reshape(count, W * W, width).astype(jnp.bfloat16)

def reference(tokens, offsets, regions, norm_gain, w_qkv, w_proj, w_merge, coarse_gain, w_in, w_out):
    lat_shift = offsets[0]
    lon_shift = offsets[1]
    rolled = jnp.roll(tokens, (-lat_shift, -lon_shift), axis=(0, 1))
    rolled_labels = jnp.roll(regions, (-lat_shift, -lon_shift), axis=(0, 1))
    strips = rolled.reshape(NLAT // W, W, NLON, C)
    strip_labels = rolled_labels.reshape(NLAT // W, W, NLON)
    columns = NLON // W

    def strip_work(pair):
        field, labels = pair
        normed = layer_norm(field, norm_gain).astype(jnp.bfloat16)
        packed = jnp.dot(normed.reshape(-1, C), w_qkv, preferred_element_type=jnp.float32).astype(jnp.bfloat16)
        packed = packed.reshape(W, columns, W, 3 * C).transpose(1, 0, 2, 3).reshape(columns, W * W, 3 * C)
        label_win = labels.reshape(W, columns, W).transpose(1, 0, 2).reshape(columns, W * W)
        mixed = attend(packed, label_win)
        return mixed.reshape(columns, W, W, C).transpose(1, 0, 2, 3).reshape(W, NLON, C)
    mixed = lax.map(strip_work, (strips, strip_labels)).reshape(NLAT, NLON, C)
    mixed = jnp.roll(mixed, (lat_shift, lon_shift), axis=(0, 1))
    update = jnp.dot(mixed.reshape(-1, C), w_proj, preferred_element_type=jnp.float32).reshape(NLAT, NLON, C)
    fine_out = (tokens.astype(jnp.float32) + update).astype(jnp.bfloat16)
    grouped = fine_out.reshape(NLAT // 2, 2, NLON // 2, 2, C).transpose(0, 2, 1, 3, 4).reshape(NLAT // 2, NLON // 2, 4 * C)

    def coarse_row(row):
        normed = plain_norm(row).astype(jnp.bfloat16)
        coarse = jnp.dot(normed, w_merge, preferred_element_type=jnp.float32).astype(jnp.bfloat16)
        coarse_normed = layer_norm(coarse, coarse_gain).astype(jnp.bfloat16)
        hidden = jax.nn.gelu(jnp.dot(coarse_normed, w_in, preferred_element_type=jnp.float32), approximate=False).astype(jnp.bfloat16)
        result = coarse.astype(jnp.float32) + jnp.dot(hidden, w_out, preferred_element_type=jnp.float32)
        return result.astype(jnp.bfloat16)
    coarse_out = lax.map(coarse_row, grouped)
    return (fine_out, coarse_out)
```

```python
import jax
import jax.numpy as jnp
import numpy as np
from jax import lax
from jax.experimental import pallas as pl
from jax.experimental.pallas import tpu as pltpu
from jax.sharding import Mesh, PartitionSpec as P

HEADS = 8
W = 8
ROWS = 16
COLS = 64
C = 512
CC = 1024
BANDS = 3
WINS = 9
F32 = jnp.float32
BF16 = jnp.bfloat16


def dot(a, b, dims=((1,), (0,))):
    return lax.dot_general(a, b, (dims, ((), ())), preferred_element_type=F32)


def norm_rows(values):
    width = values.shape[-1]
    center = values - jnp.sum(values, axis=-1, keepdims=True) * (1.0 / width)
    spread = jnp.sum(center * center, axis=-1, keepdims=True) * (1.0 / width)
    return center * lax.rsqrt(spread + 1e-05)


def fine_kernel(
    offs, own, up, down, left, right, up_c, down_c, own_lab, gain, coarse_gain,
    w_qkv_hbm, w_proj_hbm, w_merge_hbm,
    fine_out, coarse_out, normed_out,
    frame, labels, x_buf, packed, mixed, fine, grouped, w_qkv, w_proj, w_merge, sems,
):
    a = offs[0]
    b = offs[1]
    copies = [
        pltpu.make_async_copy(src, dst, sems.at[i])
        for i, (src, dst) in enumerate(
            ((w_qkv_hbm, w_qkv), (w_proj_hbm, w_proj), (w_merge_hbm, w_merge))
        )
    ]
    for copy in copies:
        copy.start()

    def turned(values, steps):
        return pltpu.roll(values, steps, axis=values.ndim - 2)

    in_turn = 8 - b
    frame[8:24, 0] = turned(left[0 : ROWS * 8, :].astype(F32).reshape(ROWS, 8, C), in_turn)
    frame[8:24, 9] = turned(right[0 : ROWS * 8, :].astype(F32).reshape(ROWS, 8, C), in_turn)
    up_v = turned(up_c[0:112, :].astype(F32).reshape(2, 7, 8, C), in_turn)
    frame[1:8, 0] = up_v[0]
    frame[1:8, 9] = up_v[1]
    down_v = turned(down_c[0:112, :].astype(F32).reshape(2, 7, 8, C), in_turn)
    frame[24:31, 0] = down_v[0]
    frame[24:31, 9] = down_v[1]

    @pl.loop(0, ROWS)
    def _(r):
        frame[8 + r, 1:9] = turned(own[r].astype(F32).reshape(8, 8, C), in_turn)

    @pl.loop(0, 7)
    def _(r):
        at = pl.multiple_of(r * COLS, COLS)
        frame[1 + r, 1:9] = turned(up[pl.ds(at, COLS), :].astype(F32).reshape(8, 8, C), in_turn)
        frame[24 + r, 1:9] = turned(
            down[pl.ds(at, COLS), :].astype(F32).reshape(8, 8, C), in_turn
        )

    labels[8:24, :] = (
        own_lab[...].astype(F32)
        + left[128:144, 0:128].astype(F32)
        + right[128:144, 0:128].astype(F32)
    )
    labels[0:8, :] = (up[448:464, 0:128].astype(F32) + up_c[112:128, 0:128].astype(F32))[8:16]
    labels[24:32, :] = (down[448:464, 0:128].astype(F32) + down_c[112:128, 0:128].astype(F32))[0:8]

    gain_v = gain[...]
    lane = lax.broadcasted_iota(jnp.int32, (64, 128), 1)
    inner_col = lax.broadcasted_iota(jnp.int32, (64, 128), 0) % 8
    low_half = lane < 64
    sub = lax.broadcasted_iota(jnp.int32, (8, 8, C), 1)
    copies[0].wait()

    @pl.loop(0, BANDS)
    def _(band):
        row = a + 8 * band

        for w in range(WINS):
            tile = jnp.where(
                sub < 8 - b, frame[pl.ds(row, 8), w], frame[pl.ds(row, 8), w + 1]
            ).reshape(64, C)
            x_buf[64 * w : 64 * w + 64, :] = (norm_rows(tile) * gain_v).astype(BF16)

        for n in range(6):
            packed[:, 256 * n : 256 * n + 256] = dot(
                x_buf[...], w_qkv[:, 256 * n : 256 * n + 256]
            ).astype(BF16)

        band_labels = labels[pl.ds(row, 8), :]
        spread = jnp.broadcast_to(band_labels[:, None, :], (8, 8, 128)).reshape(64, 128)

        @pl.loop(0, WINS)
        def _(w):
            base = pl.multiple_of(w * 64, 64)
            label = jnp.sum(
                jnp.where(lane == inner_col + (8 * w + b), spread, 0.0), axis=-1, keepdims=True
            )
            one = jnp.where(lane == 1, 1.0, 0.0)
            left_side = jnp.where(lane == 0, label, one).astype(BF16)
            right_side = jnp.where(lane == 0, 1.0, jnp.where(lane == 1, -label, 0.0)).astype(BF16)
            differ = dot(left_side, jnp.concatenate([right_side, right_side], axis=0), ((1,), (1,)))
            allowed = differ == 0.0
            outs = []
            for pair in range(HEADS // 2):
                q = packed[pl.ds(base, 64), 128 * pair : 128 * pair + 128]
                k = packed[pl.ds(base, 64), C + 128 * pair : C + 128 * pair + 128]
                v = packed[pl.ds(base, 64), 2 * C + 128 * pair : 2 * C + 128 * pair + 128]
                zero = jnp.zeros_like(q)
                both = jnp.concatenate(
                    [jnp.where(low_half, q, zero), jnp.where(low_half, zero, q)], axis=0
                )
                scores = dot(k, both, ((1,), (1,))) * 0.125
                scores = jnp.where(allowed, scores, -1e30)
                scores = scores - jnp.max(scores, axis=0, keepdims=True)
                weights = jnp.exp(scores)
                total = jnp.sum(weights, axis=0, keepdims=True)
                probs = (weights * (1.0 / total)).astype(BF16)
                result = dot(probs, v, ((0,), (0,)))
                outs.append(jnp.where(low_half, result[:64], result[64:]))
            rows = jnp.concatenate(outs, axis=-1)
            mixed[pl.ds(8 * band, 8), w] = turned(rows.reshape(8, 8, C), b)

    copies[1].wait()
    out_sub = lax.broadcasted_iota(jnp.int32, (4, 8, 8, C), 2)

    @pl.loop(0, ROWS // 4)
    def _(i):
        r = 4 * i
        across = mixed[pl.ds(8 - a + r, 4)]
        mine = jnp.where(out_sub < b, across[:, :8], across[:, 1:])
        mine = mine.reshape(4 * COLS, C).astype(BF16)
        update = dot(mine, w_proj[...])
        value = own[pl.ds(r, 4)].astype(F32).reshape(4 * COLS, C) + update
        rounded = value.astype(BF16)
        fine_out[pl.ds(r, 4)] = rounded.reshape(4, COLS, C)
        exact = rounded.astype(F32)
        for t in range(4):
            fine[t, pl.ds(r, 4)] = exact[:, 128 * t : 128 * t + 128].reshape(4, COLS, 128)

    @pl.loop(0, ROWS // 2)
    def _(i):
        parts = [
            fine[t, 2 * i + dr, pl.ds(dc, COLS // 2, stride=2), :]
            for dr in range(2)
            for dc in range(2)
            for t in range(4)
        ]
        joined = norm_rows(jnp.concatenate(parts, axis=-1))
        grouped[pl.ds(pl.multiple_of(i * 32, 32), 32), :] = joined.astype(BF16)

    copies[2].wait()
    for n in range(4):
        coarse_out[:, 256 * n : 256 * n + 256] = dot(
            grouped[...], w_merge[:, 256 * n : 256 * n + 256]
        ).astype(BF16)
    normed_out[...] = (norm_rows(coarse_out[...].astype(F32)) * coarse_gain[...]).astype(BF16)


def fine_level(offs, own, up, down, left, right, up_c, down_c, own_lab, gain, coarse_gain,
               w_qkv, w_proj, w_merge):
    vmem = pl.BlockSpec(memory_space=pltpu.VMEM)
    anywhere = pl.BlockSpec(memory_space=pl.ANY)
    return pl.pallas_call(
        fine_kernel,
        out_shape=(
            jax.ShapeDtypeStruct((ROWS, COLS, C), BF16),
            jax.ShapeDtypeStruct((256, CC), BF16),
            jax.ShapeDtypeStruct((256, CC), BF16),
        ),
        in_specs=[pl.BlockSpec(memory_space=pltpu.SMEM)] + [vmem] * 10 + [anywhere] * 3,
        out_specs=(vmem, vmem, vmem),
        scratch_shapes=[
            pltpu.VMEM((32, 10, 8, C), F32),
            pltpu.VMEM((32, 128), F32),
            pltpu.VMEM((WINS * 64, C), BF16),
            pltpu.VMEM((WINS * 64, 3 * C), BF16),
            pltpu.VMEM((24, WINS, 8, C), F32),
            pltpu.VMEM((4, ROWS, COLS, 128), F32),
            pltpu.VMEM((256, 4 * C), BF16),
            pltpu.VMEM((C, 3 * C), BF16),
            pltpu.VMEM((C, C), BF16),
            pltpu.VMEM((4 * C, CC), BF16),
            pltpu.SemaphoreType.DMA((3,)),
        ],
        compiler_params=pltpu.CompilerParams(vmem_limit_bytes=50 * 1024 * 1024),
        cost_estimate=pl.CostEstimate(
            flops=9_000_000_000, bytes_accessed=12_000_000, transcendentals=1_000_000
        ),
    )(offs, own, up, down, left, right, up_c, down_c, own_lab, gain, coarse_gain,
      w_qkv, w_proj, w_merge)


def coarse_kernel(x, w_in, w_out, out, acc):
    step = pl.program_id(0)

    @pl.when(step == 0)
    def _():
        acc[...] = jnp.zeros_like(acc)

    width = w_in.shape[-1]
    before = dot(x[...], w_in[...].reshape(CC, width))
    hidden = (0.5 * before * (1.0 + lax.erf(before * np.float32(np.sqrt(0.5))))).astype(BF16)
    acc[...] += dot(hidden, w_out[...].reshape(CC, width), ((1,), (1,)))

    @pl.when(step == pl.num_programs(0) - 1)
    def _():
        out[...] = acc[...].astype(out.dtype)


def coarse_level(x, weights, dtype):
    shards, _, depth, width = weights.shape
    block = 256
    return pl.pallas_call(
        coarse_kernel,
        grid=(width // block,),
        out_shape=jax.ShapeDtypeStruct(x.shape, dtype),
        in_specs=[
            pl.BlockSpec(x.shape, lambda n: (0, 0)),
            pl.BlockSpec((shards, 1, depth, block), lambda n: (0, 0, 0, n)),
            pl.BlockSpec((shards, 1, depth, block), lambda n: (0, 1, 0, n)),
        ],
        out_specs=pl.BlockSpec(x.shape, lambda n: (0, 0)),
        scratch_shapes=[pltpu.VMEM(x.shape, F32)],
        compiler_params=pltpu.CompilerParams(vmem_limit_bytes=40 * 1024 * 1024),
        cost_estimate=pl.CostEstimate(
            flops=4 * x.shape[0] * CC * width, bytes_accessed=10_000_000, transcendentals=0
        ),
    )(x, weights, weights)


def ring(count, step):
    return [(i, (i + step) % count) for i in range(count)]


def on_device(
    tokens, offsets, regions, norm_gain, w_qkv, w_proj, w_merge, coarse_gain, w_in, w_out
):
    rows_axes, rows_n = ("lat", "inner"), lax.axis_size(("lat", "inner"))
    cols_axes, cols_n = ("y", "x", "core"), lax.axis_size(("y", "x", "core"))
    shards = jnp.stack([w_in, w_out.T])
    weights = lax.all_gather(shards, cols_axes, axis=0, tiled=False)

    lab = regions.astype(BF16)
    own_lab = jnp.pad(lab, ((0, 0), (8, 56)))
    wide_lab = jnp.pad(own_lab, ((0, 0), (0, C - 128)))
    to_next = jnp.concatenate([tokens[9:].reshape(-1, C), wide_lab])
    to_prev = jnp.concatenate([tokens[:7].reshape(-1, C), wide_lab])
    to_right = jnp.concatenate(
        [tokens[:, 56:].reshape(-1, C), jnp.pad(lab[:, 56:], ((0, 0), (0, C - 8)))]
    )
    to_left = jnp.concatenate(
        [tokens[:, :8].reshape(-1, C), jnp.pad(lab[:, :8], ((0, 0), (72, C - 80)))]
    )
    left = lax.ppermute(to_right, cols_axes, ring(cols_n, 1))
    right = lax.ppermute(to_left, cols_axes, ring(cols_n, -1))
    up = lax.ppermute(to_next, rows_axes, ring(rows_n, 1))
    down = lax.ppermute(to_prev, rows_axes, ring(rows_n, -1))
    side_lab = left[128:] + right[128:]
    up_c = lax.ppermute(
        jnp.concatenate([left[72:128], right[72:128], side_lab]), rows_axes, ring(rows_n, 1)
    )
    down_c = lax.ppermute(
        jnp.concatenate([left[:56], right[:56], side_lab]), rows_axes, ring(rows_n, -1)
    )
    fine_out, coarse, normed = fine_level(
        offsets, tokens, up, down, left, right, up_c, down_c, own_lab,
        norm_gain.reshape(1, -1), coarse_gain.reshape(1, -1), w_qkv, w_proj, w_merge,
    )
    swap = [(0, 1), (1, 0)]
    theirs = lax.ppermute(normed, "inner", swap)
    their_part = coarse_level(theirs, weights, BF16)
    returned = lax.ppermute(their_part, "inner", swap)
    own_part = coarse_level(normed, weights, F32)
    coarse_out = (coarse.astype(F32) + own_part + returned.astype(F32)).astype(BF16)
    return fine_out, coarse_out.reshape(ROWS // 2, COLS // 2, CC)


def solution(mesh):
    fine_mesh = Mesh(
        np.array(mesh.devices).reshape(4, 4, 4, 2, 2), ("lat", "y", "x", "core", "inner")
    )
    lon = ("y", "x", "core")
    placed = (
        P(("lat", "inner"), lon, None),
        P(),
        P(("lat", "inner"), lon),
        P(),
        P(),
        P(),
        P(),
        P(),
        P(lon, "inner"),
        P("inner", lon),
    )
    return jax.shard_map(
        on_device,
        mesh=fine_mesh,
        in_specs=placed,
        out_specs=(P(("lat", "inner"), lon, None), P(("lat", "inner"), lon, None)),
        check_vma=False,
    )
```

```python
import jax
import jax.numpy as jnp
import numpy as np
from jax import lax
from jax.experimental import pallas as pl
from jax.experimental.pallas import tpu as pltpu
from jax.sharding import Mesh, PartitionSpec as P

HEADS = 8
W = 8
ROWS = 16
COLS = 64
C = 512
CC = 1024
BANDS = 3
WINS = 9
GROUP = 3
QUAD = 256
MOST = 62 * 1024 * 1024
F32 = jnp.float32
BF16 = jnp.bfloat16


def dot(a, b, dims=((1,), (0,))):
    return lax.dot_general(a, b, (dims, ((), ())), preferred_element_type=F32)


def norm_rows(values):
    width = values.shape[-1]
    center = values - jnp.sum(values, axis=-1, keepdims=True) * (1.0 / width)
    spread = jnp.sum(center * center, axis=-1, keepdims=True) * (1.0 / width)
    return center * lax.rsqrt(spread + 1e-05)


def fine_kernel(
    offs, up, down, left, right, up_c, down_c, own_lab, own_hbm, gain_hbm, coarse_gain_hbm,
    w_qkv_hbm, w_proj_hbm, w_merge_hbm,
    fine_out, coarse_out, normed_a, normed_b,
    frame, labels, x_buf, packed, mixed, fine, grouped,
    own, gain, coarse_gain, w_qkv, w_proj, w_merge, sems,
):
    a = offs[0]
    b = offs[1]
    copies = [
        pltpu.make_async_copy(src, dst, sems.at[i])
        for i, (src, dst) in enumerate(
            (
                (own_hbm, own),
                (gain_hbm, gain),
                (w_qkv_hbm, w_qkv),
                (w_proj_hbm, w_proj),
                (w_merge_hbm, w_merge),
                (coarse_gain_hbm, coarse_gain),
            )
        )
    ]
    for copy in copies:
        copy.start()

    def turned(values, steps):
        return pltpu.roll(values, steps, axis=values.ndim - 2)

    in_turn = 8 - b
    frame[8:24, 0] = turned(left[0 : ROWS * 8, :].astype(F32).reshape(ROWS, 8, C), in_turn)
    frame[8:24, 9] = turned(right[0 : ROWS * 8, :].astype(F32).reshape(ROWS, 8, C), in_turn)
    up_v = turned(up_c[0:112, :].astype(F32).reshape(2, 7, 8, C), in_turn)
    frame[1:8, 0] = up_v[0]
    frame[1:8, 9] = up_v[1]
    down_v = turned(down_c[0:112, :].astype(F32).reshape(2, 7, 8, C), in_turn)
    frame[24:31, 0] = down_v[0]
    frame[24:31, 9] = down_v[1]

    @pl.loop(0, 7)
    def _(r):
        at = pl.multiple_of(r * COLS, COLS)
        frame[1 + r, 1:9] = turned(up[pl.ds(at, COLS), :].astype(F32).reshape(8, 8, C), in_turn)
        frame[24 + r, 1:9] = turned(
            down[pl.ds(at, COLS), :].astype(F32).reshape(8, 8, C), in_turn
        )

    labels[8:24, :] = (
        own_lab[...].astype(F32)
        + left[128:144, 0:128].astype(F32)
        + right[128:144, 0:128].astype(F32)
    )
    labels[0:8, :] = (up[448:464, 0:128].astype(F32) + up_c[112:128, 0:128].astype(F32))[8:16]
    labels[24:32, :] = (down[448:464, 0:128].astype(F32) + down_c[112:128, 0:128].astype(F32))[0:8]

    copies[0].wait()

    @pl.loop(0, ROWS)
    def _(r):
        frame[8 + r, 1:9] = turned(own[r].astype(F32).reshape(8, 8, C), in_turn)

    copies[1].wait()
    gain_v = gain[...]
    lane = lax.broadcasted_iota(jnp.int32, (64, 128), 1)
    inner_col = lax.broadcasted_iota(jnp.int32, (64, 128), 0) % 8
    low_half = lane < 64
    head_lane = lax.broadcasted_iota(jnp.int32, (64, QUAD), 1) // 64
    sub = lax.broadcasted_iota(jnp.int32, (8, 8, C), 1)
    copies[2].wait()

    @pl.loop(0, BANDS)
    def _(band):
        row = a + 8 * band

        for w in range(WINS):
            tile = jnp.where(
                sub < 8 - b, frame[pl.ds(row, 8), w], frame[pl.ds(row, 8), w + 1]
            ).reshape(64, C)
            x_buf[64 * w : 64 * w + 64, :] = (norm_rows(tile) * gain_v).astype(BF16)

        for n in range(6):
            packed[:, 256 * n : 256 * n + 256] = dot(
                x_buf[...], w_qkv[:, 256 * n : 256 * n + 256]
            ).astype(BF16)

        band_labels = labels[pl.ds(row, 8), :]
        spread = jnp.broadcast_to(band_labels[:, None, :], (8, 8, 128)).reshape(64, 128)

        @pl.loop(0, WINS // GROUP)
        def _(g):
            masks, rows = [], []
            for j in range(GROUP):
                w = GROUP * g + j
                label = jnp.sum(
                    jnp.where(lane == inner_col + (8 * w + b), spread, 0.0), axis=-1, keepdims=True
                )
                one = jnp.where(lane == 1, 1.0, 0.0)
                left_side = jnp.where(lane == 0, label, one).astype(BF16)
                right_side = jnp.where(lane == 0, 1.0, jnp.where(lane == 1, -label, 0.0))
                right_side = right_side.astype(BF16)
                differ = dot(left_side, jnp.concatenate([right_side] * 4, axis=0), ((1,), (1,)))
                masks.append(differ == 0.0)
                rows.append(pl.ds(pl.multiple_of(w * 64, 64), 64))
            all_scores = []
            for j in range(GROUP):
                for part in range(2):
                    q = packed[rows[j], QUAD * part : QUAD * part + QUAD]
                    k = packed[rows[j], C + QUAD * part : C + QUAD * part + QUAD]
                    zero = jnp.zeros_like(q)
                    spread_q = jnp.concatenate(
                        [jnp.where(head_lane == h, q, zero) for h in range(4)], axis=0
                    )
                    all_scores.append(dot(k, spread_q, ((1,), (1,))))
            all_probs = []
            for j in range(GROUP):
                for part in range(2):
                    scores = jnp.where(masks[j], all_scores[2 * j + part] * 0.125, -1e30)
                    scores = scores - jnp.max(scores, axis=0, keepdims=True)
                    weights = jnp.exp(scores)
                    total = jnp.sum(weights, axis=0, keepdims=True)
                    all_probs.append((weights * (1.0 / total)).astype(BF16))
            for j in range(GROUP):
                outs = []
                for part in range(2):
                    v = packed[rows[j], 2 * C + QUAD * part : 2 * C + QUAD * part + QUAD]
                    for half in range(2):
                        result = dot(
                            all_probs[2 * j + part][:, 128 * half : 128 * half + 128],
                            v[:, 128 * half : 128 * half + 128],
                            ((0,), (0,)),
                        )
                        outs.append(jnp.where(low_half, result[:64], result[64:]))
                value = jnp.concatenate(outs, axis=-1)
                mixed[pl.ds(8 * band, 8), GROUP * g + j] = turned(value.reshape(8, 8, C), b)

    copies[3].wait()
    out_sub = lax.broadcasted_iota(jnp.int32, (4, 8, 8, C), 2)

    @pl.loop(0, ROWS // 4)
    def _(i):
        r = 4 * i
        across = mixed[pl.ds(8 - a + r, 4)]
        mine = jnp.where(out_sub < b, across[:, :8], across[:, 1:])
        mine = mine.reshape(4 * COLS, C).astype(BF16)
        update = dot(mine, w_proj[...])
        value = own[pl.ds(r, 4)].astype(F32).reshape(4 * COLS, C) + update
        rounded = value.astype(BF16)
        fine_out[pl.ds(r, 4)] = rounded.reshape(4, COLS, C)
        exact = rounded.astype(F32)
        for t in range(4):
            fine[t, pl.ds(r, 4)] = exact[:, 128 * t : 128 * t + 128].reshape(4, COLS, 128)

    @pl.loop(0, ROWS // 2)
    def _(i):
        parts = [
            fine[t, 2 * i + dr, pl.ds(dc, COLS // 2, stride=2), :]
            for dr in range(2)
            for dc in range(2)
            for t in range(4)
        ]
        joined = norm_rows(jnp.concatenate(parts, axis=-1))
        grouped[pl.ds(pl.multiple_of(i * 32, 32), 32), :] = joined.astype(BF16)

    copies[4].wait()
    for n in range(4):
        coarse_out[:, 256 * n : 256 * n + 256] = dot(
            grouped[...], w_merge[:, 256 * n : 256 * n + 256]
        ).astype(BF16)
    copies[5].wait()
    for part, out in enumerate((normed_a, normed_b)):
        rows = coarse_out[128 * part : 128 * part + 128, :].astype(F32)
        out[...] = (norm_rows(rows) * coarse_gain[...]).astype(BF16)


def pack_kernel(
    tokens, regions, to_next, to_prev, to_right, to_left, own_lab
):
    area = 7 * COLS
    label = regions[...].astype(F32)
    label = jnp.concatenate([label, jnp.zeros((ROWS, 128 - COLS), F32)], axis=-1)
    label = pltpu.roll(label, 8, axis=1)
    lane = lax.broadcasted_iota(jnp.int32, label.shape, 1)
    last = pltpu.roll(jnp.where(lane >= COLS, label, 0.0), 64, axis=1)
    last = jnp.where(lane < 8, last, 0.0)
    first = pltpu.roll(jnp.where(lane < 16, label, 0.0), 64, axis=1)
    blank = jnp.zeros((ROWS, C - 128), F32)

    def wide(part):
        return jnp.concatenate([part, blank], axis=-1).astype(BF16)

    own_lab[...] = label.astype(BF16)
    to_next[0:area, :] = tokens[9:16].reshape(area, C)
    to_next[area : area + ROWS, :] = wide(label)
    to_prev[0:area, :] = tokens[0:7].reshape(area, C)
    to_prev[area : area + ROWS, :] = wide(label)
    to_right[0:128, :] = (
        tokens[:, 48:64, :].astype(F32)[:, 8:16, :].reshape(128, C).astype(BF16)
    )
    to_right[128:144, :] = wide(last)
    to_left[0:128, :] = tokens[:, 0:16, :].astype(F32)[:, 0:8, :].reshape(128, C).astype(BF16)
    to_left[128:144, :] = wide(first)


def pack(tokens, regions):
    vmem = pl.BlockSpec(memory_space=pltpu.VMEM)
    rows = 7 * COLS + ROWS
    shapes = ((rows, C), (rows, C), (144, C), (144, C), (ROWS, 128))
    return pl.pallas_call(
        pack_kernel,
        out_shape=tuple(jax.ShapeDtypeStruct(shape, BF16) for shape in shapes),
        in_specs=[vmem] * 2,
        out_specs=(vmem,) * 5,
        compiler_params=pltpu.CompilerParams(vmem_limit_bytes=16 * 1024 * 1024),
        cost_estimate=pl.CostEstimate(flops=0, bytes_accessed=4_000_000, transcendentals=0),
    )(tokens, regions)


def fine_level(offs, up, down, left, right, up_c, down_c, own_lab, own, gain, coarse_gain,
               w_qkv, w_proj, w_merge):
    vmem = pl.BlockSpec(memory_space=pltpu.VMEM)
    anywhere = pl.BlockSpec(memory_space=pltpu.HBM)
    return pl.pallas_call(
        fine_kernel,
        out_shape=(
            jax.ShapeDtypeStruct((ROWS, COLS, C), BF16),
            jax.ShapeDtypeStruct((256, CC), BF16),
            jax.ShapeDtypeStruct((128, CC), BF16),
            jax.ShapeDtypeStruct((128, CC), BF16),
        ),
        in_specs=[pl.BlockSpec(memory_space=pltpu.SMEM)] + [vmem] * 7 + [anywhere] * 6,
        out_specs=(vmem,) * 4,
        scratch_shapes=[
            pltpu.VMEM((32, 10, 8, C), F32),
            pltpu.VMEM((32, 128), F32),
            pltpu.VMEM((WINS * 64, C), BF16),
            pltpu.VMEM((WINS * 64, 3 * C), BF16),
            pltpu.VMEM((24, WINS, 8, C), F32),
            pltpu.VMEM((4, ROWS, COLS, 128), F32),
            pltpu.VMEM((256, 4 * C), BF16),
            pltpu.VMEM((ROWS, COLS, C), BF16),
            pltpu.VMEM((1, C), F32),
            pltpu.VMEM((1, CC), F32),
            pltpu.VMEM((C, 3 * C), BF16),
            pltpu.VMEM((C, C), BF16),
            pltpu.VMEM((4 * C, CC), BF16),
            pltpu.SemaphoreType.DMA((6,)),
        ],
        compiler_params=pltpu.CompilerParams(vmem_limit_bytes=MOST),
        cost_estimate=pl.CostEstimate(
            flops=9_000_000_000, bytes_accessed=12_000_000, transcendentals=1_000_000
        ),
    )(offs, up, down, left, right, up_c, down_c, own_lab, own, gain, coarse_gain,
      w_qkv, w_proj, w_merge)


def coarse_kernel(x_a, x_b, weights, out_a, out_b, x, hidden):
    shards, _, depth, width = weights.shape
    half = x_a.shape[0]
    x[0:half, :] = x_a[...]
    x[half : 2 * half, :] = x_b[...]
    for n in range(width // 256):
        cols = slice(256 * n, 256 * n + 256)
        before = dot(x[...], weights[:, 0, :, cols].reshape(CC, 256))
        hidden[:, cols] = (
            0.5 * before * (1.0 + lax.erf(before * np.float32(np.sqrt(0.5))))
        ).astype(BF16)
    for n in range(CC // 256):
        cols = slice(256 * n, 256 * n + 256)
        span = weights[256 // depth * n : 256 // depth * (n + 1), 1].reshape(256, width)
        value = dot(hidden[...], span, ((1,), (1,))).astype(out_a.dtype)
        out_a[:, cols] = value[:half]
        out_b[:, cols] = value[half:]


def coarse_level(x_a, x_b, weights, dtype):
    width = weights.shape[-1]
    rows = x_a.shape[0]
    vmem = pl.BlockSpec(memory_space=pltpu.VMEM)
    return pl.pallas_call(
        coarse_kernel,
        out_shape=(jax.ShapeDtypeStruct(x_a.shape, dtype),) * 2,
        in_specs=[vmem] * 3,
        out_specs=(vmem, vmem),
        scratch_shapes=[
            pltpu.VMEM((2 * rows, CC), BF16),
            pltpu.VMEM((2 * rows, width), BF16),
        ],
        compiler_params=pltpu.CompilerParams(vmem_limit_bytes=40 * 1024 * 1024),
        cost_estimate=pl.CostEstimate(
            flops=8 * rows * CC * width, bytes_accessed=10_000_000, transcendentals=0
        ),
    )(x_a, x_b, weights)


def ring(count, step):
    return [(i, (i + step) % count) for i in range(count)]


def on_device(
    tokens, offsets, regions, norm_gain, w_qkv, w_proj, w_merge, coarse_gain, w_in, w_out
):
    rows_axes, rows_n = ("lat", "inner"), lax.axis_size(("lat", "inner"))
    cols_axes, cols_n = ("y", "x", "core"), lax.axis_size(("y", "x", "core"))
    weights = lax.all_gather(jnp.stack([w_in, w_out.T]), cols_axes, axis=0, tiled=False)
    to_next, to_prev, to_right, to_left, own_lab = pack(tokens, regions)
    up = lax.ppermute(to_next, rows_axes, ring(rows_n, 1))
    down = lax.ppermute(to_prev, rows_axes, ring(rows_n, -1))
    left = lax.ppermute(to_right, cols_axes, ring(cols_n, 1))
    right = lax.ppermute(to_left, cols_axes, ring(cols_n, -1))
    side_lab = left[128:] + right[128:]
    up_c = lax.ppermute(
        jnp.concatenate([left[72:128], right[72:128], side_lab]), rows_axes, ring(rows_n, 1)
    )
    down_c = lax.ppermute(
        jnp.concatenate([left[:56], right[:56], side_lab]), rows_axes, ring(rows_n, -1)
    )
    fine_out, coarse, normed_a, normed_b = fine_level(
        offsets, up, down, left, right, up_c, down_c, own_lab, tokens,
        norm_gain.reshape(1, -1), coarse_gain.reshape(1, -1), w_qkv, w_proj, w_merge,
    )
    their_a = lax.ppermute(normed_a, rows_axes, ring(rows_n, 1))
    their_b = lax.ppermute(normed_b, rows_axes, ring(rows_n, -1))
    part_a, part_b = coarse_level(their_a, their_b, weights, BF16)
    back_a = lax.ppermute(part_a, rows_axes, ring(rows_n, -1))
    back_b = lax.ppermute(part_b, rows_axes, ring(rows_n, 1))
    own_a, own_b = coarse_level(normed_a, normed_b, weights, F32)
    change = jnp.concatenate([own_a + back_a.astype(F32), own_b + back_b.astype(F32)])
    coarse_out = (coarse.astype(F32) + change).astype(BF16)
    return fine_out, coarse_out.reshape(ROWS // 2, COLS // 2, CC)


def solution(mesh):
    fine_mesh = Mesh(
        np.array(mesh.devices).reshape(4, 4, 4, 2, 2), ("lat", "y", "x", "core", "inner")
    )
    lon = ("y", "x", "core")
    placed = (
        P(("lat", "inner"), lon, None),
        P(),
        P(("lat", "inner"), lon),
        P(),
        P(),
        P(),
        P(),
        P(),
        P(lon, "inner"),
        P("inner", lon),
    )
    return jax.shard_map(
        on_device,
        mesh=fine_mesh,
        in_specs=placed,
        out_specs=(P(("lat", "inner"), lon, None), P(("lat", "inner"), lon, None)),
        check_vma=False,
    )
```

```python
import jax
import jax.numpy as jnp
import numpy as np
from jax import lax
from jax.experimental import pallas as pl
from jax.experimental.pallas import tpu as pltpu
from jax.sharding import Mesh, PartitionSpec as P

HEADS = 8
W = 8
ROWS = 16
COLS = 64
C = 512
CC = 1024
BANDS = 3
WINS = 9
GROUP = 3
QUAD = 256
MOST = 62 * 1024 * 1024
COARSE_LIMIT = 32 * 1024 * 1024
F32 = jnp.float32
BF16 = jnp.bfloat16


def dot(a, b, dims=((1,), (0,))):
    return lax.dot_general(a, b, (dims, ((), ())), preferred_element_type=F32)


def norm_rows(values):
    width = values.shape[-1]
    center = values - jnp.sum(values, axis=-1, keepdims=True) * (1.0 / width)
    spread = jnp.sum(center * center, axis=-1, keepdims=True) * (1.0 / width)
    return center * lax.rsqrt(spread + 1e-05)


def fine_kernel(
    offs, up, down, left, right, up_c, down_c, own_lab, own_hbm, gain_hbm, coarse_gain_hbm,
    w_qkv_hbm, w_proj_hbm, w_merge_hbm,
    fine_out, coarse_out, normed_a, normed_b,
    frame, labels, x_buf, packed, mixed, fine, grouped,
    own, gain, coarse_gain, w_qkv, w_proj, w_merge, sems,
):
    a = offs[0]
    b = offs[1]
    copies = [
        pltpu.make_async_copy(src, dst, sems.at[i])
        for i, (src, dst) in enumerate(
            (
                (own_hbm, own),
                (gain_hbm, gain),
                (w_qkv_hbm, w_qkv),
                (w_proj_hbm, w_proj),
                (w_merge_hbm, w_merge),
                (coarse_gain_hbm, coarse_gain),
            )
        )
    ]
    for copy in copies:
        copy.start()

    def turned(values, steps):
        return pltpu.roll(values, steps, axis=values.ndim - 2)

    in_turn = 8 - b
    frame[8:24, 0] = turned(left[0 : ROWS * 8, :].astype(F32).reshape(ROWS, 8, C), in_turn)
    frame[8:24, 9] = turned(right[0 : ROWS * 8, :].astype(F32).reshape(ROWS, 8, C), in_turn)
    up_v = turned(up_c[0:112, :].astype(F32).reshape(2, 7, 8, C), in_turn)
    frame[1:8, 0] = up_v[0]
    frame[1:8, 9] = up_v[1]
    down_v = turned(down_c[0:112, :].astype(F32).reshape(2, 7, 8, C), in_turn)
    frame[24:31, 0] = down_v[0]
    frame[24:31, 9] = down_v[1]

    @pl.loop(0, 7)
    def _(r):
        at = pl.multiple_of(r * COLS, COLS)
        frame[1 + r, 1:9] = turned(up[pl.ds(at, COLS), :].astype(F32).reshape(8, 8, C), in_turn)
        frame[24 + r, 1:9] = turned(
            down[pl.ds(at, COLS), :].astype(F32).reshape(8, 8, C), in_turn
        )

    labels[8:24, :] = (
        own_lab[...].astype(F32)
        + left[128:144, 0:128].astype(F32)
        + right[128:144, 0:128].astype(F32)
    )
    labels[0:8, :] = (up[448:464, 0:128].astype(F32) + up_c[112:128, 0:128].astype(F32))[8:16]
    labels[24:32, :] = (down[448:464, 0:128].astype(F32) + down_c[112:128, 0:128].astype(F32))[0:8]

    copies[0].wait()

    @pl.loop(0, ROWS)
    def _(r):
        frame[8 + r, 1:9] = turned(own[r].astype(F32).reshape(8, 8, C), in_turn)

    copies[1].wait()
    gain_v = gain[...]
    lane = lax.broadcasted_iota(jnp.int32, (64, 128), 1)
    inner_col = lax.broadcasted_iota(jnp.int32, (64, 128), 0) % 8
    low_half = lane < 64
    head_lane = lax.broadcasted_iota(jnp.int32, (64, QUAD), 1) // 64
    sub = lax.broadcasted_iota(jnp.int32, (8, 8, C), 1)
    copies[2].wait()

    @pl.loop(0, BANDS)
    def _(band):
        row = a + 8 * band

        for w in range(WINS):
            tile = jnp.where(
                sub < 8 - b, frame[pl.ds(row, 8), w], frame[pl.ds(row, 8), w + 1]
            ).reshape(64, C)
            x_buf[64 * w : 64 * w + 64, :] = (norm_rows(tile) * gain_v).astype(BF16)

        for n in range(6):
            packed[:, 256 * n : 256 * n + 256] = dot(
                x_buf[...], w_qkv[:, 256 * n : 256 * n + 256]
            ).astype(BF16)

        band_labels = labels[pl.ds(row, 8), :]
        spread = jnp.broadcast_to(band_labels[:, None, :], (8, 8, 128)).reshape(64, 128)

        @pl.loop(0, WINS // GROUP)
        def _(g):
            masks, rows = [], []
            for j in range(GROUP):
                w = GROUP * g + j
                label = jnp.sum(
                    jnp.where(lane == inner_col + (8 * w + b), spread, 0.0), axis=-1, keepdims=True
                )
                one = jnp.where(lane == 1, 1.0, 0.0)
                left_side = jnp.where(lane == 0, label, one).astype(BF16)
                right_side = jnp.where(lane == 0, 1.0, jnp.where(lane == 1, -label, 0.0))
                right_side = right_side.astype(BF16)
                differ = dot(left_side, jnp.concatenate([right_side] * 4, axis=0), ((1,), (1,)))
                masks.append(differ == 0.0)
                rows.append(pl.ds(pl.multiple_of(w * 64, 64), 64))
            all_scores = []
            for j in range(GROUP):
                for part in range(2):
                    q = packed[rows[j], QUAD * part : QUAD * part + QUAD]
                    k = packed[rows[j], C + QUAD * part : C + QUAD * part + QUAD]
                    zero = jnp.zeros_like(q)
                    spread_q = jnp.concatenate(
                        [jnp.where(head_lane == h, q, zero) for h in range(4)], axis=0
                    )
                    all_scores.append(dot(k, spread_q, ((1,), (1,))))
            all_probs = []
            for j in range(GROUP):
                for part in range(2):
                    scores = jnp.where(masks[j], all_scores[2 * j + part] * 0.125, -1e30)
                    scores = scores - jnp.max(scores, axis=0, keepdims=True)
                    weights = jnp.exp(scores)
                    total = jnp.sum(weights, axis=0, keepdims=True)
                    all_probs.append((weights * (1.0 / total)).astype(BF16))
            for j in range(GROUP):
                outs = []
                for part in range(2):
                    v = packed[rows[j], 2 * C + QUAD * part : 2 * C + QUAD * part + QUAD]
                    for half in range(2):
                        result = dot(
                            all_probs[2 * j + part][:, 128 * half : 128 * half + 128],
                            v[:, 128 * half : 128 * half + 128],
                            ((0,), (0,)),
                        )
                        outs.append(jnp.where(low_half, result[:64], result[64:]))
                value = jnp.concatenate(outs, axis=-1)
                mixed[pl.ds(8 * band, 8), GROUP * g + j] = turned(value.reshape(8, 8, C), b)

    copies[3].wait()
    out_sub = lax.broadcasted_iota(jnp.int32, (4, 8, 8, C), 2)

    @pl.loop(0, ROWS // 4)
    def _(i):
        r = 4 * i
        across = mixed[pl.ds(8 - a + r, 4)]
        mine = jnp.where(out_sub < b, across[:, :8], across[:, 1:])
        mine = mine.reshape(4 * COLS, C).astype(BF16)
        update = dot(mine, w_proj[...])
        value = own[pl.ds(r, 4)].astype(F32).reshape(4 * COLS, C) + update
        rounded = value.astype(BF16)
        fine_out[pl.ds(r, 4)] = rounded.reshape(4, COLS, C)
        exact = rounded.astype(F32)
        for t in range(4):
            fine[t, pl.ds(r, 4)] = exact[:, 128 * t : 128 * t + 128].reshape(4, COLS, 128)

    @pl.loop(0, ROWS // 2)
    def _(i):
        parts = [
            fine[t, 2 * i + dr, pl.ds(dc, COLS // 2, stride=2), :]
            for dr in range(2)
            for dc in range(2)
            for t in range(4)
        ]
        joined = norm_rows(jnp.concatenate(parts, axis=-1))
        grouped[pl.ds(pl.multiple_of(i * 32, 32), 32), :] = joined.astype(BF16)

    copies[4].wait()
    for n in range(4):
        coarse_out[:, 256 * n : 256 * n + 256] = dot(
            grouped[...], w_merge[:, 256 * n : 256 * n + 256]
        ).astype(BF16)
    copies[5].wait()
    for part, out in enumerate((normed_a, normed_b)):
        rows = coarse_out[128 * part : 128 * part + 128, :].astype(F32)
        out[...] = (norm_rows(rows) * coarse_gain[...]).astype(BF16)


def pack_kernel(
    tokens, regions, to_next, to_prev, to_right, to_left, own_lab
):
    area = 7 * COLS
    label = regions[...].astype(F32)
    label = jnp.concatenate([label, jnp.zeros((ROWS, 128 - COLS), F32)], axis=-1)
    label = pltpu.roll(label, 8, axis=1)
    lane = lax.broadcasted_iota(jnp.int32, label.shape, 1)
    last = pltpu.roll(jnp.where(lane >= COLS, label, 0.0), 64, axis=1)
    last = jnp.where(lane < 8, last, 0.0)
    first = pltpu.roll(jnp.where(lane < 16, label, 0.0), 64, axis=1)
    blank = jnp.zeros((ROWS, C - 128), F32)

    def wide(part):
        return jnp.concatenate([part, blank], axis=-1).astype(BF16)

    own_lab[...] = label.astype(BF16)
    to_next[0:area, :] = tokens[9:16].reshape(area, C)
    to_next[area : area + ROWS, :] = wide(label)
    to_prev[0:area, :] = tokens[0:7].reshape(area, C)
    to_prev[area : area + ROWS, :] = wide(label)
    to_right[0:128, :] = (
        tokens[:, 48:64, :].astype(F32)[:, 8:16, :].reshape(128, C).astype(BF16)
    )
    to_right[128:144, :] = wide(last)
    to_left[0:128, :] = tokens[:, 0:16, :].astype(F32)[:, 0:8, :].reshape(128, C).astype(BF16)
    to_left[128:144, :] = wide(first)


def pack(tokens, regions):
    vmem = pl.BlockSpec(memory_space=pltpu.VMEM)
    rows = 7 * COLS + ROWS
    shapes = ((rows, C), (rows, C), (144, C), (144, C), (ROWS, 128))
    return pl.pallas_call(
        pack_kernel,
        out_shape=tuple(jax.ShapeDtypeStruct(shape, BF16) for shape in shapes),
        in_specs=[vmem] * 2,
        out_specs=(vmem,) * 5,
        compiler_params=pltpu.CompilerParams(vmem_limit_bytes=16 * 1024 * 1024),
        cost_estimate=pl.CostEstimate(flops=0, bytes_accessed=4_000_000, transcendentals=0),
    )(tokens, regions)


def fine_level(offs, up, down, left, right, up_c, down_c, own_lab, own, gain, coarse_gain,
               w_qkv, w_proj, w_merge):
    vmem = pl.BlockSpec(memory_space=pltpu.VMEM)
    anywhere = pl.BlockSpec(memory_space=pltpu.HBM)
    return pl.pallas_call(
        fine_kernel,
        out_shape=(
            jax.ShapeDtypeStruct((ROWS, COLS, C), BF16),
            jax.ShapeDtypeStruct((256, CC), BF16),
            jax.ShapeDtypeStruct((128, CC), BF16),
            jax.ShapeDtypeStruct((128, CC), BF16),
        ),
        in_specs=[pl.BlockSpec(memory_space=pltpu.SMEM)] + [vmem] * 7 + [anywhere] * 6,
        out_specs=(vmem,) * 4,
        scratch_shapes=[
            pltpu.VMEM((32, 10, 8, C), F32),
            pltpu.VMEM((32, 128), F32),
            pltpu.VMEM((WINS * 64, C), BF16),
            pltpu.VMEM((WINS * 64, 3 * C), BF16),
            pltpu.VMEM((24, WINS, 8, C), F32),
            pltpu.VMEM((4, ROWS, COLS, 128), F32),
            pltpu.VMEM((256, 4 * C), BF16),
            pltpu.VMEM((ROWS, COLS, C), BF16),
            pltpu.VMEM((1, C), F32),
            pltpu.VMEM((1, CC), F32),
            pltpu.VMEM((C, 3 * C), BF16),
            pltpu.VMEM((C, C), BF16),
            pltpu.VMEM((4 * C, CC), BF16),
            pltpu.SemaphoreType.DMA((6,)),
        ],
        compiler_params=pltpu.CompilerParams(vmem_limit_bytes=MOST),
        cost_estimate=pl.CostEstimate(
            flops=9_000_000_000, bytes_accessed=12_000_000, transcendentals=1_000_000
        ),
    )(offs, up, down, left, right, up_c, down_c, own_lab, own, gain, coarse_gain,
      w_qkv, w_proj, w_merge)


def coarse_kernel(place, x_a, x_b, *rest):
    own, other, (out_a, out_b, x, hidden) = rest[:4], rest[4:8], rest[8:]
    half = x_a.shape[0]
    width = hidden.shape[-1]
    slot_x = [(x_at + 4 - place[0]) % 4 for x_at in range(4)]
    slot_y = [(y_at + 4 - place[1]) % 4 for y_at in range(4)]
    for j in range(4):
        at = pl.ds(pl.multiple_of((place[1] + j) % 4 * 256, 256), 256)
        x[0:half, 256 * j : 256 * j + 256] = x_a[:, at]
        x[half : 2 * half, 256 * j : 256 * j + 256] = x_b[:, at]

    def work(w_in, w_out):
        for n in range(width // 256):
            cols = slice(256 * n, 256 * n + 256)
            block = jnp.concatenate(
                [w_in[i // 8][slot_x[i // 2 % 4], i % 2, :, cols] for i in range(32)], axis=0
            )
            before = dot(x[...], block)
            hidden[:, cols] = (
                0.5 * before * (1.0 + lax.erf(before * np.float32(np.sqrt(0.5))))
            ).astype(BF16)
        for n in range(4):
            cols = slice(256 * n, 256 * n + 256)
            span = jnp.concatenate(
                [w_out[i // 2][slot_y[n], 1 - i % 2] for i in range(8)], axis=0
            )
            value = dot(hidden[...], span, ((1,), (1,)))
            value = pltpu.roll(value, 64 * place[0], axis=1).astype(out_a.dtype)
            out_a[:, cols] = value[:half]
            out_b[:, cols] = value[half:]

    @pl.when(place[2] == 0)
    def _():
        work(own, other)

    @pl.when(place[2] == 1)
    def _():
        work(other, own)


def coarse_level(place, x_a, x_b, pieces, dtype):
    width = pieces[0].shape[-1]
    rows = x_a.shape[0]
    vmem = pl.BlockSpec(memory_space=pltpu.VMEM)
    return pl.pallas_call(
        coarse_kernel,
        out_shape=(jax.ShapeDtypeStruct(x_a.shape, dtype),) * 2,
        in_specs=[pl.BlockSpec(memory_space=pltpu.SMEM)] + [vmem] * 10,
        out_specs=(vmem, vmem),
        scratch_shapes=[
            pltpu.VMEM((2 * rows, CC), BF16),
            pltpu.VMEM((2 * rows, width), BF16),
        ],
        compiler_params=pltpu.CompilerParams(vmem_limit_bytes=COARSE_LIMIT),
        cost_estimate=pl.CostEstimate(
            flops=8 * rows * CC * width, bytes_accessed=10_000_000, transcendentals=0
        ),
    )(place, x_a, x_b, *pieces)


def ring(count, step):
    return [(i, (i + step) % count) for i in range(count)]


def from_ahead(block, steps, second):
    pairs = []
    for y in range(4):
        for x in range(4):
            for core in range(2):
                on_x = (core == 0) != second
                source = (y, (x + steps) % 4) if on_x else ((y + steps) % 4, x)
                pairs.append(((source[0] * 4 + source[1]) * 2 + core, (y * 4 + x) * 2 + core))
    return lax.ppermute(block, ("y", "x", "core"), pairs)


def around(block, second):
    return [block] + [from_ahead(block, steps, second) for steps in (1, 3, 2)]


def on_device(
    tokens, offsets, regions, norm_gain, w_qkv, w_proj, w_merge, coarse_gain, w_in, w_out
):
    rows_axes, rows_n = ("lat", "inner"), lax.axis_size(("lat", "inner"))
    cols_axes, cols_n = ("y", "x", "core"), lax.axis_size(("y", "x", "core"))
    core = lax.axis_index("core")
    w_out = w_out.T
    keep = jnp.where(core == 0, w_in, w_out)
    give = jnp.where(core == 0, w_out, w_in)
    pair = jnp.stack([keep, lax.ppermute(give, "core", ring(2, 1))])
    to_next, to_prev, to_right, to_left, own_lab = pack(tokens, regions)
    up = lax.ppermute(to_next, rows_axes, ring(rows_n, 1))
    down = lax.ppermute(to_prev, rows_axes, ring(rows_n, -1))
    left = lax.ppermute(to_right, cols_axes, ring(cols_n, 1))
    right = lax.ppermute(to_left, cols_axes, ring(cols_n, -1))
    zero, one, three, two = around(pair, False)
    strip = jnp.stack([zero, one, two, three])
    side_lab = left[128:] + right[128:]
    up_c = lax.ppermute(
        jnp.concatenate([left[72:128], right[72:128], side_lab]), rows_axes, ring(rows_n, 1)
    )
    down_c = lax.ppermute(
        jnp.concatenate([left[:56], right[:56], side_lab]), rows_axes, ring(rows_n, -1)
    )
    zero, one, three, two = around(strip, True)
    far = [one, two, three]
    last = lax.ppermute(strip, "core", ring(2, 1))
    fine_out, coarse, normed_a, normed_b = fine_level(
        offsets, up, down, left, right, up_c, down_c, own_lab, tokens,
        norm_gain.reshape(1, -1), coarse_gain.reshape(1, -1), w_qkv, w_proj, w_merge,
    )
    far, last, normed_a, normed_b = lax.optimization_barrier((far, last, normed_a, normed_b))
    swapped = [lax.ppermute(piece, "core", ring(2, 1)) for piece in far]
    pieces = [strip] + far + [last] + swapped
    their_a = lax.ppermute(normed_a, rows_axes, ring(rows_n, 1))
    their_b = lax.ppermute(normed_b, rows_axes, ring(rows_n, -1))
    place = jnp.stack([lax.axis_index("x"), lax.axis_index("y"), core])
    part_a, part_b = coarse_level(place, their_a, their_b, pieces, BF16)
    back_a = lax.ppermute(part_a, rows_axes, ring(rows_n, -1))
    back_b = lax.ppermute(part_b, rows_axes, ring(rows_n, 1))
    own_a, own_b = coarse_level(place, normed_a, normed_b, pieces, F32)
    change = jnp.concatenate([own_a + back_a.astype(F32), own_b + back_b.astype(F32)])
    coarse_out = (coarse.astype(F32) + change).astype(BF16)
    return fine_out, coarse_out.reshape(ROWS // 2, COLS // 2, CC)


def solution(mesh):
    fine_mesh = Mesh(
        np.array(mesh.devices).reshape(4, 4, 4, 2, 2), ("lat", "y", "x", "core", "inner")
    )
    lon = ("y", "x", "core")
    placed = (
        P(("lat", "inner"), lon, None),
        P(),
        P(("lat", "inner"), lon),
        P(),
        P(),
        P(),
        P(),
        P(),
        P(lon, "inner"),
        P("inner", lon),
    )
    return jax.shard_map(
        on_device,
        mesh=fine_mesh,
        in_specs=placed,
        out_specs=(P(("lat", "inner"), lon, None), P(("lat", "inner"), lon, None)),
        check_vma=False,
    )
```

```python
import jax
import jax.numpy as jnp
import numpy as np
from jax import lax
from jax.experimental import pallas as pl
from jax.experimental.pallas import tpu as pltpu
from jax.sharding import Mesh, PartitionSpec as P

HEADS = 8
W = 8
ROWS = 16
COLS = 64
C = 512
CC = 1024
BANDS = 3
WINS = 9
GROUP = 9
QUAD = 256
MOST = 62 * 1024 * 1024
COARSE_LIMIT = 32 * 1024 * 1024
F32 = jnp.float32
BF16 = jnp.bfloat16


def dot(a, b, dims=((1,), (0,))):
    return lax.dot_general(a, b, (dims, ((), ())), preferred_element_type=F32)


def norm_rows(values):
    width = values.shape[-1]
    center = values - jnp.sum(values, axis=-1, keepdims=True) * (1.0 / width)
    spread = jnp.sum(center * center, axis=-1, keepdims=True) * (1.0 / width)
    return center * lax.rsqrt(spread + 1e-05)


def fine_kernel(
    offs, up, down, left, right, up_c, down_c, own_lab, own_hbm, gain_hbm, coarse_gain_hbm,
    w_qkv_hbm, w_proj_hbm, w_merge_hbm,
    fine_out, coarse_out, normed_a, normed_b,
    frame, labels, x_buf, packed, mixed, fine, grouped,
    own, gain, coarse_gain, w_qkv, w_proj, w_merge, sems,
):
    a = offs[0]
    b = offs[1]
    copies = [
        pltpu.make_async_copy(src, dst, sems.at[i])
        for i, (src, dst) in enumerate(
            (
                (own_hbm, own),
                (gain_hbm, gain),
                (w_qkv_hbm, w_qkv),
                (w_proj_hbm, w_proj),
                (w_merge_hbm, w_merge),
                (coarse_gain_hbm, coarse_gain),
            )
        )
    ]
    for copy in copies:
        copy.start()

    def turned(values, steps):
        return pltpu.roll(values, steps, axis=values.ndim - 2)

    in_turn = 8 - b
    frame[8:24, 0] = turned(left[0 : ROWS * 8, :].astype(F32).reshape(ROWS, 8, C), in_turn)
    frame[8:24, 9] = turned(right[0 : ROWS * 8, :].astype(F32).reshape(ROWS, 8, C), in_turn)
    up_v = turned(up_c[0:112, :].astype(F32).reshape(2, 7, 8, C), in_turn)
    frame[1:8, 0] = up_v[0]
    frame[1:8, 9] = up_v[1]
    down_v = turned(down_c[0:112, :].astype(F32).reshape(2, 7, 8, C), in_turn)
    frame[24:31, 0] = down_v[0]
    frame[24:31, 9] = down_v[1]

    @pl.loop(0, 7, unroll=7)
    def _(r):
        at = pl.multiple_of(r * COLS, COLS)
        frame[1 + r, 1:9] = turned(up[pl.ds(at, COLS), :].astype(F32).reshape(8, 8, C), in_turn)
        frame[24 + r, 1:9] = turned(
            down[pl.ds(at, COLS), :].astype(F32).reshape(8, 8, C), in_turn
        )

    labels[8:24, :] = (
        own_lab[...].astype(F32)
        + left[128:144, 0:128].astype(F32)
        + right[128:144, 0:128].astype(F32)
    )
    labels[0:8, :] = (up[448:464, 0:128].astype(F32) + up_c[112:128, 0:128].astype(F32))[8:16]
    labels[24:32, :] = (down[448:464, 0:128].astype(F32) + down_c[112:128, 0:128].astype(F32))[0:8]

    copies[0].wait()

    @pl.loop(0, ROWS, unroll=4)
    def _(r):
        frame[8 + r, 1:9] = turned(own[r].astype(F32).reshape(8, 8, C), in_turn)

    copies[1].wait()
    gain_v = gain[...]
    lane = lax.broadcasted_iota(jnp.int32, (64, 128), 1)
    inner_col = lax.broadcasted_iota(jnp.int32, (64, 128), 0) % 8
    low_half = lane < 64
    head_lane = lax.broadcasted_iota(jnp.int32, (64, QUAD), 1) // 64
    sub = lax.broadcasted_iota(jnp.int32, (8, 8, C), 1)
    copies[2].wait()

    @pl.loop(0, BANDS)
    def _(band):
        row = a + 8 * band

        for w in range(WINS):
            tile = jnp.where(
                sub < 8 - b, frame[pl.ds(row, 8), w], frame[pl.ds(row, 8), w + 1]
            ).reshape(64, C)
            x_buf[64 * w : 64 * w + 64, :] = (norm_rows(tile) * gain_v).astype(BF16)

        for n in range(6):
            packed[:, 256 * n : 256 * n + 256] = dot(
                x_buf[...], w_qkv[:, 256 * n : 256 * n + 256]
            ).astype(BF16)

        band_labels = labels[pl.ds(row, 8), :]
        spread = jnp.broadcast_to(band_labels[:, None, :], (8, 8, 128)).reshape(64, 128)

        @pl.loop(0, WINS // GROUP)
        def _(g):
            masks, rows = [], []
            for j in range(GROUP):
                w = GROUP * g + j
                label = jnp.sum(
                    jnp.where(lane == inner_col + (8 * w + b), spread, 0.0), axis=-1, keepdims=True
                )
                one = jnp.where(lane == 1, 1.0, 0.0)
                left_side = jnp.where(lane == 0, label, one).astype(BF16)
                right_side = jnp.where(lane == 0, 1.0, jnp.where(lane == 1, -label, 0.0))
                right_side = right_side.astype(BF16)
                differ = dot(left_side, jnp.concatenate([right_side] * 4, axis=0), ((1,), (1,)))
                masks.append(differ == 0.0)
                rows.append(pl.ds(pl.multiple_of(w * 64, 64), 64))
            all_scores = []
            for j in range(GROUP):
                for part in range(2):
                    q = packed[rows[j], QUAD * part : QUAD * part + QUAD]
                    k = packed[rows[j], C + QUAD * part : C + QUAD * part + QUAD]
                    zero = jnp.zeros_like(q)
                    spread_q = jnp.concatenate(
                        [jnp.where(head_lane == h, q, zero) for h in range(4)], axis=0
                    )
                    all_scores.append(dot(k, spread_q, ((1,), (1,))))
            all_probs = []
            for j in range(GROUP):
                for part in range(2):
                    scores = jnp.where(masks[j], all_scores[2 * j + part] * 0.125, -1e30)
                    scores = scores - jnp.max(scores, axis=0, keepdims=True)
                    weights = jnp.exp(scores)
                    total = jnp.sum(weights, axis=0, keepdims=True)
                    all_probs.append((weights * (1.0 / total)).astype(BF16))
            for j in range(GROUP):
                outs = []
                for part in range(2):
                    v = packed[rows[j], 2 * C + QUAD * part : 2 * C + QUAD * part + QUAD]
                    for half in range(2):
                        result = dot(
                            all_probs[2 * j + part][:, 128 * half : 128 * half + 128],
                            v[:, 128 * half : 128 * half + 128],
                            ((0,), (0,)),
                        )
                        outs.append(jnp.where(low_half, result[:64], result[64:]))
                value = jnp.concatenate(outs, axis=-1)
                mixed[pl.ds(8 * band, 8), GROUP * g + j] = turned(value.reshape(8, 8, C), b)

    copies[3].wait()
    out_sub = lax.broadcasted_iota(jnp.int32, (4, 8, 8, C), 2)

    @pl.loop(0, ROWS // 4, unroll=2)
    def _(i):
        r = 4 * i
        across = mixed[pl.ds(8 - a + r, 4)]
        mine = jnp.where(out_sub < b, across[:, :8], across[:, 1:])
        mine = mine.reshape(4 * COLS, C).astype(BF16)
        update = dot(mine, w_proj[...])
        value = own[pl.ds(r, 4)].astype(F32).reshape(4 * COLS, C) + update
        rounded = value.astype(BF16)
        fine_out[pl.ds(r, 4)] = rounded.reshape(4, COLS, C)
        exact = rounded.astype(F32)
        for t in range(4):
            fine[t, pl.ds(r, 4)] = exact[:, 128 * t : 128 * t + 128].reshape(4, COLS, 128)

    @pl.loop(0, ROWS // 2, unroll=4)
    def _(i):
        parts = [
            fine[t, 2 * i + dr, pl.ds(dc, COLS // 2, stride=2), :]
            for dr in range(2)
            for dc in range(2)
            for t in range(4)
        ]
        joined = norm_rows(jnp.concatenate(parts, axis=-1))
        grouped[pl.ds(pl.multiple_of(i * 32, 32), 32), :] = joined.astype(BF16)

    copies[4].wait()
    for n in range(4):
        coarse_out[:, 256 * n : 256 * n + 256] = dot(
            grouped[...], w_merge[:, 256 * n : 256 * n + 256]
        ).astype(BF16)
    copies[5].wait()
    for part, out in enumerate((normed_a, normed_b)):
        rows = coarse_out[128 * part : 128 * part + 128, :].astype(F32)
        out[...] = (norm_rows(rows) * coarse_gain[...]).astype(BF16)


def pack_kernel(
    tokens, regions, to_next, to_prev, to_right, to_left, own_lab
):
    area = 7 * COLS
    label = regions[...].astype(F32)
    label = jnp.concatenate([label, jnp.zeros((ROWS, 128 - COLS), F32)], axis=-1)
    label = pltpu.roll(label, 8, axis=1)
    lane = lax.broadcasted_iota(jnp.int32, label.shape, 1)
    last = pltpu.roll(jnp.where(lane >= COLS, label, 0.0), 64, axis=1)
    last = jnp.where(lane < 8, last, 0.0)
    first = pltpu.roll(jnp.where(lane < 16, label, 0.0), 64, axis=1)
    blank = jnp.zeros((ROWS, C - 128), F32)

    def wide(part):
        return jnp.concatenate([part, blank], axis=-1).astype(BF16)

    own_lab[...] = label.astype(BF16)
    to_next[0:area, :] = tokens[9:16].reshape(area, C)
    to_next[area : area + ROWS, :] = wide(label)
    to_prev[0:area, :] = tokens[0:7].reshape(area, C)
    to_prev[area : area + ROWS, :] = wide(label)
    to_right[0:128, :] = (
        tokens[:, 48:64, :].astype(F32)[:, 8:16, :].reshape(128, C).astype(BF16)
    )
    to_right[128:144, :] = wide(last)
    to_left[0:128, :] = tokens[:, 0:16, :].astype(F32)[:, 0:8, :].reshape(128, C).astype(BF16)
    to_left[128:144, :] = wide(first)


def pack(tokens, regions):
    vmem = pl.BlockSpec(memory_space=pltpu.VMEM)
    rows = 7 * COLS + ROWS
    shapes = ((rows, C), (rows, C), (144, C), (144, C), (ROWS, 128))
    return pl.pallas_call(
        pack_kernel,
        out_shape=tuple(jax.ShapeDtypeStruct(shape, BF16) for shape in shapes),
        in_specs=[vmem] * 2,
        out_specs=(vmem,) * 5,
        compiler_params=pltpu.CompilerParams(vmem_limit_bytes=16 * 1024 * 1024),
        cost_estimate=pl.CostEstimate(flops=0, bytes_accessed=4_000_000, transcendentals=0),
    )(tokens, regions)


def fine_level(offs, up, down, left, right, up_c, down_c, own_lab, own, gain, coarse_gain,
               w_qkv, w_proj, w_merge):
    vmem = pl.BlockSpec(memory_space=pltpu.VMEM)
    anywhere = pl.BlockSpec(memory_space=pltpu.HBM)
    return pl.pallas_call(
        fine_kernel,
        out_shape=(
            jax.ShapeDtypeStruct((ROWS, COLS, C), BF16),
            jax.ShapeDtypeStruct((256, CC), BF16),
            jax.ShapeDtypeStruct((128, CC), BF16),
            jax.ShapeDtypeStruct((128, CC), BF16),
        ),
        in_specs=[pl.BlockSpec(memory_space=pltpu.SMEM)] + [vmem] * 7 + [anywhere] * 6,
        out_specs=(vmem,) * 4,
        scratch_shapes=[
            pltpu.VMEM((32, 10, 8, C), F32),
            pltpu.VMEM((32, 128), F32),
            pltpu.VMEM((WINS * 64, C), BF16),
            pltpu.VMEM((WINS * 64, 3 * C), BF16),
            pltpu.VMEM((24, WINS, 8, C), F32),
            pltpu.VMEM((4, ROWS, COLS, 128), F32),
            pltpu.VMEM((256, 4 * C), BF16),
            pltpu.VMEM((ROWS, COLS, C), BF16),
            pltpu.VMEM((1, C), F32),
            pltpu.VMEM((1, CC), F32),
            pltpu.VMEM((C, 3 * C), BF16),
            pltpu.VMEM((C, C), BF16),
            pltpu.VMEM((4 * C, CC), BF16),
            pltpu.SemaphoreType.DMA((6,)),
        ],
        compiler_params=pltpu.CompilerParams(vmem_limit_bytes=MOST),
        cost_estimate=pl.CostEstimate(
            flops=9_000_000_000, bytes_accessed=12_000_000, transcendentals=1_000_000
        ),
    )(offs, up, down, left, right, up_c, down_c, own_lab, own, gain, coarse_gain,
      w_qkv, w_proj, w_merge)


def coarse_kernel(place, x_a, x_b, *rest):
    own, other, (out_a, out_b, x, hidden) = rest[:4], rest[4:8], rest[8:]
    half = x_a.shape[0]
    width = hidden.shape[-1]
    slot_x = [(x_at + 4 - place[0]) % 4 for x_at in range(4)]
    slot_y = [(y_at + 4 - place[1]) % 4 for y_at in range(4)]
    for j in range(4):
        at = pl.ds(pl.multiple_of((place[1] + j) % 4 * 256, 256), 256)
        x[0:half, 256 * j : 256 * j + 256] = x_a[:, at]
        x[half : 2 * half, 256 * j : 256 * j + 256] = x_b[:, at]

    def work(w_in, w_out):
        for n in range(width // 256):
            cols = slice(256 * n, 256 * n + 256)
            block = jnp.concatenate(
                [w_in[i // 8][slot_x[i // 2 % 4], i % 2, :, cols] for i in range(32)], axis=0
            )
            before = dot(x[...], block)
            hidden[:, cols] = (
                0.5 * before * (1.0 + lax.erf(before * np.float32(np.sqrt(0.5))))
            ).astype(BF16)
        for n in range(4):
            cols = slice(256 * n, 256 * n + 256)
            span = jnp.concatenate(
                [w_out[i // 2][slot_y[n], 1 - i % 2] for i in range(8)], axis=0
            )
            value = dot(hidden[...], span, ((1,), (1,)))
            value = pltpu.roll(value, 64 * place[0], axis=1).astype(out_a.dtype)
            out_a[:, cols] = value[:half]
            out_b[:, cols] = value[half:]

    @pl.when(place[2] == 0)
    def _():
        work(own, other)

    @pl.when(place[2] == 1)
    def _():
        work(other, own)


def coarse_level(place, x_a, x_b, pieces, dtype):
    width = pieces[0].shape[-1]
    rows = x_a.shape[0]
    vmem = pl.BlockSpec(memory_space=pltpu.VMEM)
    return pl.pallas_call(
        coarse_kernel,
        out_shape=(jax.ShapeDtypeStruct(x_a.shape, dtype),) * 2,
        in_specs=[pl.BlockSpec(memory_space=pltpu.SMEM)] + [vmem] * 10,
        out_specs=(vmem, vmem),
        scratch_shapes=[
            pltpu.VMEM((2 * rows, CC), BF16),
            pltpu.VMEM((2 * rows, width), BF16),
        ],
        compiler_params=pltpu.CompilerParams(vmem_limit_bytes=COARSE_LIMIT),
        cost_estimate=pl.CostEstimate(
            flops=8 * rows * CC * width, bytes_accessed=10_000_000, transcendentals=0
        ),
    )(place, x_a, x_b, *pieces)


def ring(count, step):
    return [(i, (i + step) % count) for i in range(count)]


def from_ahead(block, steps, second):
    pairs = []
    for y in range(4):
        for x in range(4):
            for core in range(2):
                on_x = (core == 0) != second
                source = (y, (x + steps) % 4) if on_x else ((y + steps) % 4, x)
                pairs.append(((source[0] * 4 + source[1]) * 2 + core, (y * 4 + x) * 2 + core))
    return lax.ppermute(block, ("y", "x", "core"), pairs)


def around(block, second):
    return [block] + [from_ahead(block, steps, second) for steps in (1, 3, 2)]


def on_device(
    tokens, offsets, regions, norm_gain, w_qkv, w_proj, w_merge, coarse_gain, w_in, w_out
):
    rows_axes, rows_n = ("lat", "inner"), lax.axis_size(("lat", "inner"))
    cols_axes, cols_n = ("y", "x", "core"), lax.axis_size(("y", "x", "core"))
    core = lax.axis_index("core")
    w_out = w_out.T
    keep = jnp.where(core == 0, w_in, w_out)
    give = jnp.where(core == 0, w_out, w_in)
    pair = jnp.stack([keep, lax.ppermute(give, "core", ring(2, 1))])
    to_next, to_prev, to_right, to_left, own_lab = pack(tokens, regions)
    up = lax.ppermute(to_next, rows_axes, ring(rows_n, 1))
    down = lax.ppermute(to_prev, rows_axes, ring(rows_n, -1))
    left = lax.ppermute(to_right, cols_axes, ring(cols_n, 1))
    right = lax.ppermute(to_left, cols_axes, ring(cols_n, -1))
    zero, one, three, two = around(pair, False)
    strip = jnp.stack([zero, one, two, three])
    side_lab = left[128:] + right[128:]
    up_c = lax.ppermute(
        jnp.concatenate([left[72:128], right[72:128], side_lab]), rows_axes, ring(rows_n, 1)
    )
    down_c = lax.ppermute(
        jnp.concatenate([left[:56], right[:56], side_lab]), rows_axes, ring(rows_n, -1)
    )
    strip, up, down = lax.optimization_barrier((strip, up, down))
    zero, one, three, two = around(strip, True)
    far = [one, two, three]
    last = lax.ppermute(strip, "core", ring(2, 1))
    fine_out, coarse, normed_a, normed_b = fine_level(
        offsets, up, down, left, right, up_c, down_c, own_lab, tokens,
        norm_gain.reshape(1, -1), coarse_gain.reshape(1, -1), w_qkv, w_proj, w_merge,
    )
    far, last, coarse = lax.optimization_barrier((far, last, coarse))
    swapped = [lax.ppermute(piece, "core", ring(2, 1)) for piece in far]
    pieces = [strip] + far + [last] + swapped
    their_a = lax.ppermute(normed_a, rows_axes, ring(rows_n, 1))
    their_b = lax.ppermute(normed_b, rows_axes, ring(rows_n, -1))
    place = jnp.stack([lax.axis_index("x"), lax.axis_index("y"), core])
    part_a, part_b = coarse_level(place, their_a, their_b, pieces, BF16)
    back_a = lax.ppermute(part_a, rows_axes, ring(rows_n, -1))
    back_b = lax.ppermute(part_b, rows_axes, ring(rows_n, 1))
    own_a, own_b = coarse_level(place, normed_a, normed_b, pieces, F32)
    change = jnp.concatenate([own_a + back_a.astype(F32), own_b + back_b.astype(F32)])
    coarse_out = (coarse.astype(F32) + change).astype(BF16)
    return fine_out, coarse_out.reshape(ROWS // 2, COLS // 2, CC)


def solution(mesh):
    fine_mesh = Mesh(
        np.array(mesh.devices).reshape(4, 4, 4, 2, 2), ("lat", "y", "x", "core", "inner")
    )
    lon = ("y", "x", "core")
    placed = (
        P(("lat", "inner"), lon, None),
        P(),
        P(("lat", "inner"), lon),
        P(),
        P(),
        P(),
        P(),
        P(),
        P(lon, "inner"),
        P("inner", lon),
    )
    return jax.shard_map(
        on_device,
        mesh=fine_mesh,
        in_specs=placed,
        out_specs=(P(("lat", "inner"), lon, None), P(("lat", "inner"), lon, None)),
        check_vma=False,
    )
```
